256 devices in a mesh: src: 16 (over z, x_hi), tgt: 16 (over x_lo, y, core).
Axes of the slice: x: 4 (x_hi: 2, x_lo: 2; x = x_hi * 2 + x_lo), y: 4, z: 8, core: 2. Of those that a mesh axis runs over, the one named last changes fastest.
Arguments:
- src_emb: bfloat16 [64, 32768], P(None, 'src'), may hold values from -2.75 to 2.75
- tgt_emb: bfloat16 [64, 131072], P(None, 'tgt'), may hold values from -2.75 to 2.75
- target_features: bfloat16 [128, 131072], P(None, 'tgt'), may hold values from -6 to 6
- src_mass: float32 [32768], P('src'), may hold values from 1 to 10
- tgt_mass: float32 [131072], P('tgt'), may hold values from 1 to 10
- kept_blocks: int32 [128, 128], P('src', 'tgt'), may hold values from 0 to 31, as said below
- kept_count: int32 [128, 16], P('src', 'tgt'), may hold values from 1 to 8
Outputs:
- projected: float32 [32768, 128], P(('src', 'tgt'))
- src_potential: float32 [32768], P('src')
- tgt_potential: float32 [131072], P('tgt')
The draws below stay inside these ranges and needn't reach their ends.
Inputs may be any that keep to these rules, and one draw needn't show every extreme that they name: `kept_blocks`: entry [r, t * 8 + k] is a block number within target shard t; the 8 entries of one group are distinct; the first kept_count[r, t] of them are kept, the others are unused; every target block is kept by some source block row.
All inputs are finite; a program needn't handle non-finite values.
Results may differ from the reference program's by a relative error of at most 0.00075.
Values sent between devices are 32-bit elements; how exact they have to be, the bound alone decides.
A program may use at most 64 MiB of HBM per device.

```python
import math
import jax
import jax.numpy as jnp
from jax import lax

DIM = 64
FEAT = 128
BLOCK = 256
KSH = 8
ITERS = 2
TGT_DEV = 8192
NS = 32768
NT = 131072
NSB = 128
TBD = 32
N_TGT = 16


def embedding_pair(key):
    base = jax.random.fold_in(key, 37)
    keys = jax.random.split(base, 7)
    src_values = 0.125 * jnp.clip(jax.random.normal(keys[0], (DIM, NS), jnp.float32), -4.0, 4.0)
    tgt_values = 0.125 * jnp.clip(jax.random.normal(keys[1], (DIM, NT), jnp.float32), -4.0, 4.0)
    strength = jax.random.uniform(keys[5], (1, NS), jnp.float32, 1.0, 1.5)
    signs = jnp.where(jax.random.uniform(keys[6], (1, NS), jnp.float32) < 0.5, -1.0, 1.0)
    far_cells = (jnp.arange(NS, dtype=jnp.int32) % 16 == 7)[None, :]
    src_values = jnp.where(far_cells, src_values + strength * signs, src_values)
    src_values = jnp.clip(src_values, -2.75, 2.75)
    tgt_values = jnp.clip(tgt_values, -2.75, 2.75)
    return (src_values, tgt_values)


def draw_src_emb(key, part):
    return embedding_pair(key)[0].astype(jnp.bfloat16)


def draw_tgt_emb(key, part):
    return embedding_pair(key)[1].astype(jnp.bfloat16)


def draw_kept_blocks(key, part):
    base = jax.random.fold_in(key, 11)
    shards = NT // TGT_DEV
    scores = jax.random.randint(base, (NSB, shards, TBD - 1), 0, 1 << 20, jnp.int32) * (TBD - 1)
    scores = scores + jnp.arange(TBD - 1, dtype=jnp.int32)
    order = (jnp.argsort(scores, axis=-1)[:, :, :KSH - 1] + 1).astype(jnp.int32)
    block_displacements = jnp.concatenate([jnp.zeros((NSB, shards, 1), jnp.int32), order], axis=-1)
    rows = jnp.arange(NSB, dtype=jnp.int32)
    blocks = (rows[:, None, None] + block_displacements) % TBD
    return blocks.reshape(NSB, shards * KSH).astype(jnp.int32)


def draw_kept_count(key, part):
    base = jax.random.fold_in(key, 23)
    keys = jax.random.split(base, 3)
    shards = NT // TGT_DEV
    shape = (NSB, shards)
    lower = jnp.minimum(jax.random.randint(keys[0], shape, 0, KSH, jnp.int32), jax.random.randint(keys[1], shape, 0, KSH, jnp.int32)) + 1
    heavy = jax.random.randint(keys[2], shape, 0, 4, jnp.int32) == 0
    leading = (jnp.arange(NSB, dtype=jnp.int32)[:, None] == 0) & (jnp.arange(shards, dtype=jnp.int32)[None, :] == 0)
    return jnp.where(heavy | leading, KSH, lower).astype(jnp.int32)


def block_levels(own_key, dims, cuts, least, top_value):
    factor_of = 1.0
    for axis_at, parts in cuts:
        draws = jax.random.uniform(jax.random.fold_in(jax.random.fold_in(own_key, 6), axis_at), (parts,), jnp.float32, least / len(cuts), top_value / len(cuts))
        factor_of = factor_of * jnp.repeat(jnp.exp(draws), dims[axis_at] // parts).reshape((-1,) + (1,) * (len(dims) - 1 - axis_at))
    return factor_of


def gaussian(own_key, shape, spread, bound, cuts=(), kind=jnp.bfloat16):
    values = jax.random.normal(own_key, shape, jnp.float32) * spread
    if len(cuts) > 0:
        values = block_levels(own_key, shape, cuts, -0.22, 0.18) * values
    return jnp.clip(values, min=-bound, max=bound).astype(kind)


def setup_inputs(seed: int = 0) -> dict:
    streams_of = jax.random.split(jax.random.key(seed), 8)
    src_emb = draw_src_emb(jax.random.fold_in(streams_of[7], 71), 0)
    tgt_emb = draw_tgt_emb(jax.random.fold_in(streams_of[7], 71), 0)
    target_features = gaussian(streams_of[2], (FEAT, NT), 1.0, 6.0, ((1, 16),))
    src_mass = jnp.clip(jnp.exp(math.log(10.0) - 2.3025851 * jax.random.uniform(streams_of[3], (NS,), jnp.float32) ** block_levels(streams_of[3], (NS,), ((0, 16),), -0.2, 0.2)), 1.0, 10.0)
    tgt_mass = jnp.clip(jnp.exp(math.log(10.0) - 2.3025851 * jax.random.uniform(streams_of[4], (NT,), jnp.float32) ** block_levels(streams_of[4], (NT,), ((0, 16),), -0.2, 0.2)), 1.0, 10.0)
    kept_blocks = draw_kept_blocks(jax.random.fold_in(streams_of[7], 71), 0)
    kept_count = draw_kept_count(jax.random.fold_in(streams_of[7], 71), 0)
    return {"src_emb": src_emb, "tgt_emb": tgt_emb, "target_features": target_features, "src_mass": src_mass, "tgt_mass": tgt_mass, "kept_blocks": kept_blocks, "kept_count": kept_count}


SENTINEL = -1.0e30
EPSILON = 0.1


def reference(src_emb, tgt_emb, target_features, src_mass, tgt_mass, kept_blocks, kept_count):
    every_block_list = N_TGT * TBD
    src_float = src_emb.astype(jnp.float32)
    tgt_float = tgt_emb.astype(jnp.float32)
    src_tiles = src_float.reshape(DIM, NSB, BLOCK).transpose(1, 0, 2)
    src_norm = jnp.sum(jnp.square(src_float), axis=0).reshape(NSB, BLOCK)
    tgt_tiles = tgt_float.reshape(DIM, every_block_list, BLOCK)
    target_norm = jnp.sum(jnp.square(tgt_float), axis=0).reshape(every_block_list, BLOCK)
    feat_tiles = target_features.astype(jnp.float32).reshape(FEAT, every_block_list, BLOCK)
    slot_ids = jnp.arange(N_TGT * KSH, dtype=jnp.int32)
    global_index = (kept_blocks + (slot_ids // KSH) * TBD).astype(jnp.int32)
    live_slot = (slot_ids % KSH)[None, :] < jnp.repeat(kept_count, KSH, axis=1)
    packets = (src_tiles, src_norm, global_index, live_slot)

    def distances(packet):
        products = jnp.einsum("dr,dkc->krc", packet[0], jnp.take(tgt_tiles, packet[2], axis=1))
        return packet[1][None, :, None] + jnp.take(target_norm, packet[2], axis=0)[:, None, :] - 2.0 * products

    def row_scaled(potential_tiles, packet):
        scaled = (jnp.take(potential_tiles, packet[2], axis=0)[:, None, :] - distances(packet)) / EPSILON
        return jnp.where(packet[3][:, None, None], scaled, SENTINEL)

    def row_pass(potential):
        potential_tiles = potential.reshape(every_block_list, BLOCK)

        def per_block(packet):
            scaled = row_scaled(potential_tiles, packet)
            highest = jnp.max(scaled, axis=(0, 2))
            totals = jnp.sum(jnp.where(packet[3][:, None, None], jnp.exp(scaled - highest[None, :, None]), 0.0), axis=(0, 2))
            return highest + jnp.log(totals)

        return lax.map(per_block, packets).reshape(NS)

    def column_pass(potential):
        potential_tiles = potential.reshape(NSB, BLOCK)

        def per_block(carry, packet):
            block_top, block_sum = carry
            scaled = (packet[4][None, :, None] - distances(packet)) / EPSILON
            scaled = jnp.where(packet[3][:, None, None], scaled, SENTINEL)
            highest = jnp.max(scaled, axis=1)
            totals = jnp.sum(jnp.where(packet[3][:, None, None], jnp.exp(scaled - highest[:, None, :]), 0.0), axis=1)
            new_top = block_top.at[packet[2]].max(highest)
            rescaled = block_sum * jnp.exp(block_top - new_top)
            added = rescaled.at[packet[2]].add(totals * jnp.exp(highest - jnp.take(new_top, packet[2], axis=0)))
            return (new_top, added), None

        start = (jnp.full((every_block_list, BLOCK), SENTINEL, jnp.float32), jnp.zeros((every_block_list, BLOCK), jnp.float32))
        (block_top, block_sum), discarded_value = lax.scan(per_block, start, packets + (potential_tiles,))
        return (block_top + jnp.log(block_sum)).reshape(NT)

    tgt_potential = jnp.zeros((NT,), jnp.float32)
    src_potential = jnp.zeros((NS,), jnp.float32)
    for iteration in range(ITERS):
        src_potential = EPSILON * jnp.log(src_mass) - EPSILON * row_pass(tgt_potential)
        tgt_potential = EPSILON * jnp.log(tgt_mass) - EPSILON * column_pass(src_potential)

    final_tiles = tgt_potential.reshape(every_block_list, BLOCK)

    def plan_block(packet):
        scaled = row_scaled(final_tiles, packet).reshape(N_TGT, KSH, BLOCK, BLOCK)
        live = packet[3].reshape(N_TGT, KSH)
        shard_top = jnp.max(scaled, axis=(1, 3))
        weights = jnp.where(live[:, :, None, None], jnp.exp(scaled - shard_top[:, None, :, None]), 0.0)
        rounded_count = lax.optimization_barrier(weights.astype(jnp.bfloat16)).astype(jnp.float32)
        feature_matrix = jnp.take(feat_tiles, packet[2], axis=1).reshape(FEAT, N_TGT, KSH, BLOCK)
        partial_numerator = jnp.einsum("pmsx,hpmx->psh", rounded_count, feature_matrix)
        shard_den = jnp.sum(rounded_count, axis=(1, 3))
        top = jnp.max(shard_top, axis=0)
        factor = jnp.exp(shard_top - top[None, :])
        numerator = jnp.sum(partial_numerator * factor[:, :, None], axis=0)
        denominator = jnp.sum(shard_den * factor, axis=0)
        return numerator / denominator[:, None]

    projected = lax.map(plan_block, packets).reshape(NS, FEAT)
    return projected, src_potential, tgt_potential
```

```python
import functools
import math

import jax
import jax.numpy as jnp
from jax import lax
from jax.experimental import pallas as pl
from jax.experimental.pallas import tpu as pltpu
from jax.sharding import PartitionSpec as P

MESH = pl.DeviceIdType.MESH
F32 = jnp.float32
BF16 = jnp.bfloat16

BLOCK = 256
DEPTH = 256
LANES = 128
EPSILON = 0.1
LN2 = math.log(2.0)
SCALE = 1.0 / (EPSILON * LN2)
ABSENT = -1e30
STRIP = 64
TINY = 2.0**-120


def split3(x):
    high = x.astype(BF16).astype(F32)
    rest = x - high
    middle = rest.astype(BF16).astype(F32)
    return high, middle, rest - middle


def iota(shape, dim):
    return lax.broadcasted_iota(jnp.int32, shape, dim)


def dot(a, b):
    return jnp.dot(a, b, preferred_element_type=F32)


def dot_nt(a, b):
    return lax.dot_general(a, b, (((1,), (1,)), ((), ())), preferred_element_type=F32)


def kernel(
    n_src,
    n_tgt,
    kb_ref,
    kc_ref,
    src_ref,
    tgt_ref,
    feat_ref,
    smass_ref,
    tmass_ref,
    proj_ref,
    spot_ref,
    tpot_ref,
    lhs,
    rhs,
    feats,
    plan,
    hot,
    member,
    slots,
    tnorm,
    vpot,
    rows_out,
    rows_in,
    cols_out,
    cols_in,
    back,
    rowtile,
    dens,
    pair_out,
    pair_own,
    pair_in,
    final_in,
    row_send,
    row_recv,
    col_send,
    col_recv,
    back_send,
    back_recv,
    pair_send,
    pair_recv,
    final_send,
    final_recv,
):
    depth = src_ref.shape[0]
    row_blocks = src_ref.shape[1] // BLOCK
    col_blocks = tgt_ref.shape[1] // BLOCK
    slot_count = kb_ref.shape[1]
    all_slots = row_blocks * slot_count
    own_blocks = col_blocks // n_src
    feat = feat_ref.shape[0]
    half = BLOCK // 2

    me_s = lax.axis_index("src")
    me_t = lax.axis_index("tgt")
    chip = me_t // 2
    core = me_t % 2

    barrier = pltpu.get_barrier_semaphore()

    def greet(axis, count, me):
        def body(o, carry):
            pl.semaphore_signal(
                barrier, inc=1, device_id={axis: lax.rem(me + o, count)}, device_id_type=MESH
            )
            return carry

        lax.fori_loop(1, count, body, 0)

    greet("tgt", n_tgt, me_t)
    greet("src", n_src, me_s)

    def row_copy(phase, peer, landing):
        return pltpu.make_async_remote_copy(
            src_ref=rows_out.at[phase],
            dst_ref=rows_in.at[phase, landing],
            send_sem=row_send.at[phase, peer],
            recv_sem=row_recv.at[phase, landing],
            device_id={"tgt": peer},
            device_id_type=MESH,
        )

    def col_copy(phase, peer, landing):
        return pltpu.make_async_remote_copy(
            src_ref=cols_out.at[phase, peer],
            dst_ref=cols_in.at[phase, landing],
            send_sem=col_send.at[phase, peer],
            recv_sem=col_recv.at[phase, landing],
            device_id={"src": peer},
            device_id_type=MESH,
        )

    def back_copy(phase, peer, origin):
        return pltpu.make_async_remote_copy(
            src_ref=back.at[phase, origin],
            dst_ref=back.at[phase, origin],
            send_sem=back_send.at[phase, peer],
            recv_sem=back_recv.at[phase, origin],
            device_id={"src": peer},
            device_id_type=MESH,
        )

    def others(count, me, act):
        def body(o, carry):
            act(lax.rem(me + o, count))
            return carry

        lax.fori_loop(1, count, body, 0)

    def slot_block(r, k):
        return jnp.where(k < kc_ref[r, 0], kb_ref[r, k], col_blocks)

    def v_tile(v):
        high, middle, low = split3(v)
        line = iota((16, BLOCK), 0)
        tile = jnp.where(line < 8, 1.0, 0.0)
        tile = jnp.where(line == 8, high, tile)
        tile = jnp.where(line == 9, middle, tile)
        return jnp.where(line == 10, low, tile).astype(BF16)

    def target_side(s, carry):
        for j in range(own_blocks):
            b = s * own_blocks + j
            y = tgt_ref[:, pl.ds(pl.multiple_of(b * BLOCK, BLOCK), BLOCK)]
            for part in range(3):
                rhs[b, part * depth : (part + 1) * depth, :] = y
            y = y.astype(F32)
            norm = jnp.sum(y * y, axis=0, keepdims=True)
            tnorm[s, j : j + 1, :] = norm
            v = norm * (-SCALE)
            vpot[s, j : j + 1, :] = v
            rhs[b, 3 * depth : 3 * depth + 16, :] = jnp.ones((16, BLOCK), BF16)
            rhs[b, 3 * depth + 16 : 3 * depth + 32, :] = v_tile(v)
            rhs[b, 3 * depth + 32 :, :] = jnp.zeros((DEPTH - 3 * depth - 32, BLOCK), BF16)
        return carry

    lax.fori_loop(0, n_src, target_side, 0)
    rhs[col_blocks, 0 : 3 * depth, :] = jnp.zeros((3 * depth, BLOCK), BF16)
    rhs[col_blocks, 3 * depth : 3 * depth + 16, :] = jnp.ones((16, BLOCK), BF16)
    rhs[col_blocks, 3 * depth + 16 : 3 * depth + 32, :] = v_tile(jnp.full((1, BLOCK), ABSENT, F32))
    rhs[col_blocks, 3 * depth + 32 :, :] = jnp.zeros((DEPTH - 3 * depth - 32, BLOCK), BF16)

    def source_side(r, carry):
        x = src_ref[:, pl.ds(pl.multiple_of(r * BLOCK, BLOCK), BLOCK)].astype(F32)
        line = iota((STRIP, BLOCK), 0)
        strip = jnp.where((line >= 24) & (line < 27), 1.0, 0.0)
        parts = jnp.concatenate([*split3(x * (2.0 * SCALE)), strip], axis=0)
        lhs[r] = parts.T.astype(BF16)
        return carry

    lax.fori_loop(0, row_blocks, source_side, 0)

    def fold(total):
        return total[:, :LANES] + total[:, LANES:]

    def first_rows(r, carry):
        left = lhs[r]
        highest = None
        for k in range(slot_count):
            z = dot(left, rhs[slot_block(r, k)])
            plan[k] = z
            peak = jnp.maximum(z[:, :LANES], z[:, LANES:])
            highest = peak if highest is None else jnp.maximum(highest, peak)
        total = None
        for k in range(slot_count):
            z = plan[k]
            e = jnp.exp2(z[:, :LANES] - highest) + jnp.exp2(z[:, LANES:] - highest)
            total = e if total is None else total + e
        highest, total = highest.T, total.T
        top = jnp.max(highest, axis=0, keepdims=True)
        total = jnp.sum(total * jnp.exp2(highest - top), axis=0, keepdims=True)
        rows_out[0, pl.ds(r, 1), :] = top + jnp.log2(total)
        return carry

    lax.fori_loop(0, row_blocks, first_rows, 0)

    pl.semaphore_wait(barrier, n_src + n_tgt - 2)

    others(n_tgt, me_t, lambda p: row_copy(0, p, me_t).start())
    rows_in[0, me_t] = rows_out[0]

    lane = iota((1, DEPTH), 1)
    lane_slot = lax.rem(lane, all_slots)

    def list_slot(i, kept):
        block = slot_block(i // slot_count, lax.rem(i, slot_count))
        return jnp.where(lane_slot == i, block, kept)

    kept = lax.fori_loop(0, all_slots, list_slot, jnp.full((1, DEPTH), col_blocks, jnp.int32))
    kept = jnp.where(lane < 3 * all_slots, kept, col_blocks)
    wide = (row_blocks * col_blocks, DEPTH)
    line = iota(wide, 0)
    chosen = (kept == lax.rem(line, col_blocks)) & (lane_slot // slot_count == line // col_blocks)
    hot[...] = jnp.where(chosen, 1.0, 0.0).astype(BF16)
    member[...] = jnp.where(kept == iota((col_blocks, DEPTH), 0), 1.0, 0.0).astype(BF16)

    def feature_side(b, carry):
        feats[b, :feat, :] = feat_ref[:, pl.ds(pl.multiple_of(b * BLOCK, BLOCK), BLOCK)]
        feats[b, feat:, :] = jnp.ones((feats.shape[1] - feat, BLOCK), BF16)
        return carry

    lax.fori_loop(0, col_blocks, feature_side, 0)

    def row_lines(ref):
        return jnp.concatenate(
            [ref[:, r * BLOCK : (r + 1) * BLOCK] for r in range(row_blocks)], axis=0
        )

    smass = row_lines(smass_ref)
    own_width = own_blocks * BLOCK
    tmass = tmass_ref[:, pl.ds(pl.multiple_of(me_s * own_width, own_width), own_width)]
    tmass = jnp.concatenate(
        [tmass[:, j * BLOCK : (j + 1) * BLOCK] for j in range(own_blocks)], axis=0
    )

    others(n_tgt, me_t, lambda p: row_copy(0, p, p).wait_recv())
    row_lse = rows_in[0]
    top = jnp.max(row_lse, axis=0)
    u = jnp.log2(smass) - top - jnp.log2(jnp.sum(jnp.exp2(row_lse - top[None]), axis=0))
    strips = jnp.concatenate(
        [
            jnp.zeros((STRIP, BLOCK), F32),
            *split3(u),
            jnp.zeros((LANES - STRIP - 3 * row_blocks, BLOCK), F32),
        ],
        axis=0,
    )
    rowtile[...] = strips.T

    def first_columns(r, carry):
        at = iota((BLOCK, LANES), 1) - STRIP
        spot = (at == r) | (at == r + row_blocks) | (at == r + 2 * row_blocks)
        old = lhs[r, :, LANES:].astype(F32)
        lhs[r, :, LANES:] = jnp.where(spot, rowtile[...], old).astype(BF16)
        left = lhs[r]
        for k in range(slot_count):
            z = dot(left, rhs[slot_block(r, k)])
            highest = jnp.max(z, axis=0, keepdims=True)
            total = jnp.sum(jnp.exp2(z - highest), axis=0, keepdims=True)
            slots[r, k : k + 1, :] = highest + jnp.log2(total)
        return carry

    lax.fori_loop(0, row_blocks, first_columns, 0)

    def slot_parts():
        lines = slots[...].reshape(all_slots, BLOCK)
        parts = [*split3(lines)]
        if 3 * all_slots < DEPTH:
            parts.append(jnp.zeros((DEPTH - 3 * all_slots, BLOCK), F32))
        return jnp.concatenate(parts, axis=0).astype(BF16)

    def send_columns(phase, lines):
        for s in range(n_src):
            cols_out[phase, s] = lines[s * own_blocks : (s + 1) * own_blocks, :]
        others(n_src, me_s, lambda p: col_copy(phase, p, me_s).start())
        cols_in[phase, me_s] = cols_out[phase, me_s]
        others(n_src, me_s, lambda p: col_copy(phase, p, p).wait_recv())

    def send_back(phase, lines):
        back[phase, me_s] = lines
        others(n_src, me_s, lambda p: back_copy(phase, p, me_s).start())

    def wait_back(phase):
        others(n_src, me_s, lambda p: back_copy(phase, p, p).wait_recv())

    present = dot(hot[...], jnp.where(iota((DEPTH, BLOCK), 0) < all_slots, 1.0, 0.0).astype(BF16))
    by_row = jnp.where(present > 0.5, dot(hot[...], slot_parts()), ABSENT)
    by_row = by_row.reshape(row_blocks, col_blocks, BLOCK)
    top = jnp.max(by_row, axis=0)
    send_columns(0, top + jnp.log2(jnp.sum(jnp.exp2(by_row - top[None]), axis=0)))
    col_lse = cols_in[0]
    top = jnp.max(col_lse, axis=0)
    total = jnp.sum(jnp.exp2(col_lse - top[None]), axis=0)
    send_back(0, vpot[me_s] + jnp.log2(tmass) - top - jnp.log2(total))
    wait_back(0)

    def new_potential(s, carry):
        for j in range(own_blocks):
            rhs[s * own_blocks + j, 3 * depth + 16 : 3 * depth + 32, :] = v_tile(
                back[0, s, j : j + 1, :]
            )
        return carry

    lax.fori_loop(0, n_src, new_potential, 0)

    def second_rows(r, carry):
        left = lhs[r]
        total = None
        for k in range(slot_count):
            e = jnp.exp2(dot(left, rhs[slot_block(r, k)]))
            plan[r * slot_count + k] = e
            total = fold(e) if total is None else total + fold(e)
        rows_out[1, pl.ds(r, 1), :] = jnp.sum(total.T, axis=0, keepdims=True)
        return carry

    lax.fori_loop(0, row_blocks, second_rows, 0)
    others(n_tgt, me_t, lambda p: row_copy(1, p, me_t).start())
    rows_in[1, me_t] = rows_out[1]
    snorm = []
    for r in range(row_blocks):
        x = src_ref[:, r * BLOCK : (r + 1) * BLOCK].astype(F32)
        snorm.append(jnp.sum(x * x, axis=0, keepdims=True))
    snorm = jnp.concatenate(snorm, axis=0)
    others(n_tgt, me_t, lambda p: row_copy(1, p, p).wait_recv())
    row_factor = smass / jnp.sum(rows_in[1], axis=0)
    rowtile[...] = jnp.concatenate(
        [row_factor, jnp.zeros((LANES - row_blocks, BLOCK), F32)], axis=0
    ).T

    def second_columns(r, carry):
        at = iota((BLOCK, LANES), 1)
        factor = jnp.sum(jnp.where(at == r, rowtile[...], 0.0), axis=1, keepdims=True)
        for k in range(slot_count):
            e = plan[r * slot_count + k]
            slots[r, k : k + 1, :] = jnp.sum(e * factor, axis=0, keepdims=True)
        return carry

    lax.fori_loop(0, row_blocks, second_columns, 0)
    send_columns(1, dot(member[...], slot_parts()))
    send_back(1, tmass / jnp.sum(cols_in[1], axis=0))
    source_potential = (EPSILON * LN2) * (u + jnp.log2(row_factor)) + snorm
    for r in range(row_blocks):
        spot_ref[:, r * BLOCK : (r + 1) * BLOCK] = source_potential[r : r + 1, :]
    wait_back(1)

    def pair_copy(step):
        return pltpu.make_async_remote_copy(
            src_ref=pair_out.at[step],
            dst_ref=pair_in.at[step],
            send_sem=pair_send.at[step],
            recv_sem=pair_recv.at[step],
            device_id={"tgt": chip * 2 + 1 - core},
            device_id_type=MESH,
        )

    def final_copy(step, r, origin):
        return pltpu.make_async_remote_copy(
            src_ref=pair_own.at[step],
            dst_ref=final_in.at[origin],
            send_sem=final_send.at[step],
            recv_sem=final_recv.at[origin],
            device_id={"tgt": r * 2 + core},
            device_id_type=MESH,
        )

    diagonal = iota((half, LANES), 0) == iota((half, LANES), 1)

    def weigh(step, r):
        highest = None
        for k in range(slot_count):
            b = kb_ref[r, k]
            factor = back[1, b // own_blocks, pl.ds(lax.rem(b, own_blocks), 1), :]
            w = plan[r * slot_count + k] * factor
            plan[r * slot_count + k] = w
            peak = jnp.maximum(w[:, :LANES], w[:, LANES:])
            highest = peak if highest is None else jnp.maximum(highest, peak)
        top = jnp.maximum(jnp.max(highest, axis=1, keepdims=True), TINY)
        scale = 1.0 / top
        total = None
        for k in range(slot_count):
            w = (plan[r * slot_count + k] * scale).astype(BF16)
            part = dot_nt(w, feats[kb_ref[r, k]])
            total = part if total is None else total + part
        total = total * top
        for h in range(2):
            sums = total[h * half : (h + 1) * half]
            den = jnp.sum(jnp.where(diagonal, sums[:, LANES:], 0.0), axis=0, keepdims=True)
            rowtile[h * half : (h + 1) * half, :] = sums[:, :LANES]
            dens[h] = jnp.broadcast_to(den, (8, LANES))

        own = pl.ds(pl.multiple_of(core * half, half), half)
        other = pl.ds(pl.multiple_of((1 - core) * half, half), half)
        pair_out[step, :half, :] = rowtile[other, :]
        pair_out[step, half:, :] = dens[1 - core]
        pair_own[step, :half, :] = rowtile[own, :]
        pair_own[step, half:, :] = dens[core]
        pair_copy(step).start()

    def share(step):
        return lax.rem(chip + 1 + step, row_blocks)

    def forward(step):
        pair_copy(step).wait_recv()
        pair_own[step] = pair_own[step] + pair_in[step]
        final_copy(step, share(step), chip).start()

    weigh(0, share(0))

    def project(step, carry):
        weigh(step, share(step))
        forward(step - 1)
        return carry

    lax.fori_loop(1, row_blocks, project, 0)
    last = row_blocks - 1
    pair_copy(last).wait_recv()
    total = pair_own[last] + pair_in[last]

    def target_out(s, carry):
        for j in range(own_blocks):
            v = back[0, s, j : j + 1, :] + jnp.log2(back[1, s, j : j + 1, :])
            at = pl.ds(pl.multiple_of((s * own_blocks + j) * BLOCK, BLOCK), BLOCK)
            tpot_ref[:, at] = (EPSILON * LN2) * v + tnorm[s, j : j + 1, :]
        return carry

    lax.fori_loop(0, n_src, target_out, 0)

    def collect(step, total):
        origin = share(step)
        final_copy(step, origin, origin).wait_recv()
        return total + final_in[origin]

    total = lax.fori_loop(0, last, collect, total)
    den = jnp.sum(jnp.where(diagonal, total[half : half + 1, :], 0.0), axis=1, keepdims=True)
    proj_ref[...] = total[:half, :] / den

    for phase in range(2):
        others(n_tgt, me_t, lambda p: row_copy(phase, p, me_t).wait_send())
        others(n_src, me_s, lambda p: col_copy(phase, p, me_s).wait_send())
        others(n_src, me_s, lambda p: back_copy(phase, p, me_s).wait_send())

    def drain(step, carry):
        pair_copy(step).wait_send()
        final_copy(step, share(step), chip).wait_send()
        return carry

    lax.fori_loop(0, last, drain, 0)
    pair_copy(last).wait_send()


def shards(n_src, n_tgt, src_emb, tgt_emb, features, src_mass, tgt_mass, kept_blocks, kept_count):
    src_rows, tgt_rows = src_emb.shape[1], tgt_emb.shape[1]
    row_blocks, col_blocks = src_rows // BLOCK, tgt_rows // BLOCK
    slot_count = kept_blocks.shape[1]
    own_blocks = col_blocks // n_src
    share_rows = src_rows // n_tgt
    feat = features.shape[0]
    vmem = pl.BlockSpec(memory_space=pltpu.VMEM)
    smem = pl.BlockSpec(memory_space=pltpu.SMEM)
    message = (row_blocks, share_rows + 8, LANES)
    dma = pltpu.SemaphoreType.DMA
    projected, src_potential, tgt_potential = pl.pallas_call(
        functools.partial(kernel, n_src, n_tgt),
        out_shape=(
            jax.ShapeDtypeStruct((share_rows, feat), F32),
            jax.ShapeDtypeStruct((1, src_rows), F32),
            jax.ShapeDtypeStruct((1, tgt_rows), F32),
        ),
        in_specs=[smem, smem, vmem, vmem, vmem, vmem, vmem],
        out_specs=(vmem, vmem, vmem),
        scratch_shapes=[
            pltpu.VMEM((row_blocks, BLOCK, DEPTH), BF16),
            pltpu.VMEM((col_blocks + 1, DEPTH, BLOCK), BF16),
            pltpu.VMEM((col_blocks, 2 * LANES, BLOCK), BF16),
            pltpu.VMEM((row_blocks * slot_count, BLOCK, BLOCK), F32),
            pltpu.VMEM((row_blocks * col_blocks, DEPTH), BF16),
            pltpu.VMEM((col_blocks, DEPTH), BF16),
            pltpu.VMEM((row_blocks, slot_count, BLOCK), F32),
            pltpu.VMEM((n_src, own_blocks, BLOCK), F32),
            pltpu.VMEM((n_src, own_blocks, BLOCK), F32),
            pltpu.VMEM((2, row_blocks, BLOCK), F32),
            pltpu.VMEM((2, n_tgt, row_blocks, BLOCK), F32),
            pltpu.VMEM((2, n_src, own_blocks, BLOCK), F32),
            pltpu.VMEM((2, n_src, own_blocks, BLOCK), F32),
            pltpu.VMEM((2, n_src, own_blocks, BLOCK), F32),
            pltpu.VMEM((BLOCK, LANES), F32),
            pltpu.VMEM((2, 8, LANES), F32),
            pltpu.VMEM(message, F32),
            pltpu.VMEM(message, F32),
            pltpu.VMEM(message, F32),
            pltpu.VMEM(message, F32),
            dma((2, n_tgt)),
            dma((2, n_tgt)),
            dma((2, n_src)),
            dma((2, n_src)),
            dma((2, n_src)),
            dma((2, n_src)),
            dma((row_blocks,)),
            dma((row_blocks,)),
            dma((row_blocks,)),
            dma((row_blocks,)),
        ],
        compiler_params=pltpu.CompilerParams(
            collective_id=0, has_side_effects=True, vmem_limit_bytes=56 * 1024 * 1024
        ),
        name="transport",
    )(
        kept_blocks,
        kept_count,
        src_emb,
        tgt_emb,
        features,
        src_mass.reshape(1, src_rows),
        tgt_mass.reshape(1, tgt_rows),
    )
    return projected, src_potential.reshape(src_rows), tgt_potential.reshape(tgt_rows)


def solution(mesh):
    return jax.shard_map(
        functools.partial(shards, mesh.shape["src"], mesh.shape["tgt"]),
        mesh=mesh,
        in_specs=(
            P(None, "src"),
            P(None, "tgt"),
            P(None, "tgt"),
            P("src"),
            P("tgt"),
            P("src", "tgt"),
            P("src", "tgt"),
        ),
        out_specs=(P(("src", "tgt"), None), P("src"), P("tgt")),
        check_vma=False,
    )
```

```python
import functools
import math

import jax
import jax.numpy as jnp
from jax import lax
from jax.experimental import pallas as pl
from jax.experimental.pallas import tpu as pltpu
from jax.sharding import PartitionSpec as P

MESH = pl.DeviceIdType.MESH
F32 = jnp.float32
BF16 = jnp.bfloat16

BLOCK = 256
DEPTH = 256
LANES = 128
EPSILON = 0.1
LN2 = math.log(2.0)
SCALE = 1.0 / (EPSILON * LN2)
ABSENT = -1e30
STRIP = 64
TINY = 2.0**-120
PLANES = 2
ROW_PARTS = 2
LAG = 2


def split3(x):
    high = x.astype(BF16).astype(F32)
    rest = x - high
    middle = rest.astype(BF16).astype(F32)
    return high, middle, rest - middle


def iota(shape, dim):
    return lax.broadcasted_iota(jnp.int32, shape, dim)


def dot(a, b):
    return jnp.dot(a, b, preferred_element_type=F32)


def dot_nt(a, b):
    return lax.dot_general(a, b, (((1,), (1,)), ((), ())), preferred_element_type=F32)


def kernel(
    n_src,
    n_tgt,
    kb_hbm,
    kc_hbm,
    src_hbm,
    tgt_hbm,
    feat_hbm,
    smass_hbm,
    tmass_hbm,
    sums_ref,
    spot_ref,
    tpot_ref,
    kb_ref,
    kc_ref,
    src_ref,
    tgt_ref,
    feat_ref,
    smass_ref,
    tmass_ref,
    lhs,
    rhs,
    feats,
    scores,
    plan,
    hot,
    member,
    slots,
    peaks,
    factors,
    norms,
    u_ref,
    first_out,
    first_in,
    second_out,
    second_in,
    cols_out,
    cols_in,
    back,
    rowtile,
    dens,
    pair_out,
    pair_own,
    pair_in,
    final_in,
    load_sem,
    first_send,
    first_recv,
    second_send,
    second_recv,
    col_send,
    col_recv,
    back_send,
    back_recv,
    pair_send,
    pair_recv,
    final_send,
    final_recv,
):
    depth = src_ref.shape[0]
    row_blocks = src_ref.shape[1] // BLOCK
    col_blocks = tgt_ref.shape[1] // BLOCK
    slot_count = kb_ref.shape[1]
    all_slots = row_blocks * slot_count
    owners = n_src // PLANES
    own_blocks = col_blocks // owners
    feat = feat_ref.shape[0]
    half = BLOCK // 2
    row_parts, part_rows = first_out.shape[0], first_out.shape[1]

    me_s = lax.axis_index("src")
    me_t = lax.axis_index("tgt")
    owner, plane = me_s // PLANES, me_s % PLANES
    chip, core = me_t // 2, me_t % 2

    barrier = pltpu.get_barrier_semaphore()

    def others(count, me, act):
        def body(i, carry):
            act((me + count // 2 + (i + 1) // 2 * (2 * (i % 2) - 1)) % count)
            return carry

        lax.fori_loop(0, count - 1, body, 0)

    def greet(axis, peer):
        pl.semaphore_signal(barrier, inc=1, device_id={axis: peer}, device_id_type=MESH)

    others(n_src, me_s, lambda p: greet("src", p))
    others(n_tgt, me_t, lambda p: greet("tgt", p))

    sources = (src_hbm, tgt_hbm, kb_hbm, kc_hbm, feat_hbm, smass_hbm, tmass_hbm)
    targets = (src_ref, tgt_ref, kb_ref, kc_ref, feat_ref, smass_ref, tmass_ref)
    loads = [
        pltpu.make_async_copy(a, b, load_sem.at[i]) for i, (a, b) in enumerate(zip(sources, targets))
    ]
    for load in loads:
        load.start()

    def first_copy(part, peer, landing):
        return pltpu.make_async_remote_copy(
            src_ref=first_out.at[part],
            dst_ref=first_in.at[part, landing],
            send_sem=first_send.at[part, peer],
            recv_sem=first_recv.at[part, landing],
            device_id={"tgt": peer},
            device_id_type=MESH,
        )

    def second_copy(peer, landing):
        return pltpu.make_async_remote_copy(
            src_ref=second_out,
            dst_ref=second_in.at[landing],
            send_sem=second_send.at[peer],
            recv_sem=second_recv.at[landing],
            device_id={"tgt": peer},
            device_id_type=MESH,
        )

    def col_copy(phase, peer, landing):
        return pltpu.make_async_remote_copy(
            src_ref=cols_out.at[phase, peer // PLANES],
            dst_ref=cols_in.at[phase, landing],
            send_sem=col_send.at[phase, peer],
            recv_sem=col_recv.at[phase, landing],
            device_id={"src": peer},
            device_id_type=MESH,
        )

    def back_copy(phase, peer, origin):
        return pltpu.make_async_remote_copy(
            src_ref=back.at[phase, origin],
            dst_ref=back.at[phase, origin],
            send_sem=back_send.at[phase, peer],
            recv_sem=back_recv.at[phase, origin],
            device_id={"src": peer * PLANES + plane},
            device_id_type=MESH,
        )

    def slot_block(r, k):
        return jnp.where(k < kc_ref[0, r], kb_ref[r, k], col_blocks)

    def v_tile(v):
        high, middle, low = split3(v)
        line = iota((16, BLOCK), 0)
        tile = jnp.where(line < 8, 1.0, 0.0)
        tile = jnp.where(line == 8, high, tile)
        tile = jnp.where(line == 9, middle, tile)
        return jnp.where(line == 10, low, tile).astype(BF16)

    loads[0].wait()

    def source_side(r, carry):
        x = src_ref[:, pl.ds(pl.multiple_of(r * BLOCK, BLOCK), BLOCK)].astype(F32)
        line = iota((STRIP, BLOCK), 0)
        strip = jnp.where((line >= 24) & (line < 27), 1.0, 0.0)
        parts = jnp.concatenate([*split3(x * (2.0 * SCALE)), strip], axis=0)
        lhs[r] = parts.T.astype(BF16)
        return carry

    lax.fori_loop(0, row_blocks, source_side, 0)

    loads[1].wait()

    def target_side(s, carry):
        for j in range(own_blocks):
            b = s * own_blocks + j
            y = tgt_ref[:, pl.ds(pl.multiple_of(b * BLOCK, BLOCK), BLOCK)]
            for part in range(3):
                rhs[b, part * depth : (part + 1) * depth, :] = y
            y = y.astype(F32)
            norm = jnp.sum(y * y, axis=0, keepdims=True)
            norms[s, j : j + 1, :] = norm
            rhs[b, 3 * depth : 3 * depth + 16, :] = jnp.ones((16, BLOCK), BF16)
            rhs[b, 3 * depth + 16 : 3 * depth + 32, :] = v_tile(norm * (-SCALE))
            rhs[b, 3 * depth + 32 :, :] = jnp.zeros((DEPTH - 3 * depth - 32, BLOCK), BF16)
        return carry

    lax.fori_loop(0, owners, target_side, 0)
    rhs[col_blocks, 0 : 3 * depth, :] = jnp.zeros((3 * depth, BLOCK), BF16)
    rhs[col_blocks, 3 * depth : 3 * depth + 16, :] = jnp.ones((16, BLOCK), BF16)
    rhs[col_blocks, 3 * depth + 16 : 3 * depth + 32, :] = v_tile(jnp.full((1, BLOCK), ABSENT, F32))
    rhs[col_blocks, 3 * depth + 32 :, :] = jnp.zeros((DEPTH - 3 * depth - 32, BLOCK), BF16)

    loads[2].wait()
    loads[3].wait()

    def first_rows(r, carry):
        left = lhs[r]
        highest = None
        for k in range(slot_count):
            z = dot(left, rhs[slot_block(r, k)])
            scores[k] = z
            peak = jnp.maximum(z[:, :LANES], z[:, LANES:])
            highest = peak if highest is None else jnp.maximum(highest, peak)
        total = None
        for k in range(slot_count):
            z = scores[k]
            e = jnp.exp2(z[:, :LANES] - highest) + jnp.exp2(z[:, LANES:] - highest)
            total = e if total is None else total + e
        highest, total = highest.T, total.T
        top = jnp.max(highest, axis=0, keepdims=True)
        total = jnp.sum(total * jnp.exp2(highest - top), axis=0, keepdims=True)
        first_out[r // part_rows, pl.ds(r % part_rows, 1), :] = top + jnp.log2(total)
        return carry

    for part in range(row_parts):
        lax.fori_loop(part * part_rows, (part + 1) * part_rows, first_rows, 0)
        if part == 0:
            pl.semaphore_wait(barrier, n_src + n_tgt - 2)
        others(n_tgt, me_t, lambda p: first_copy(part, p, me_t).start())
        first_in[part, me_t] = first_out[part]

    lane = iota((1, DEPTH), 1)
    lane_slot = lane & (all_slots - 1)

    def list_slot(i, kept):
        block = slot_block(i // slot_count, i % slot_count)
        return jnp.where(lane_slot == i, block, kept)

    kept = lax.fori_loop(0, all_slots, list_slot, jnp.full((1, DEPTH), col_blocks, jnp.int32))
    kept = jnp.where(lane < 3 * all_slots, kept, col_blocks)
    member[...] = jnp.where(kept == iota((col_blocks, DEPTH), 0), 1.0, 0.0).astype(BF16)
    for r in range(row_blocks):
        here = (lane_slot >= r * slot_count) & (lane_slot < (r + 1) * slot_count)
        mine = jnp.where(here, kept, col_blocks)
        hot[r * col_blocks : (r + 1) * col_blocks, :] = jnp.where(
            mine == iota((col_blocks, DEPTH), 0), 1.0, 0.0
        ).astype(BF16)
    u_ref[...] = jnp.zeros_like(u_ref)
    loads[5].wait()
    loads[6].wait()

    def first_columns(r, carry):
        at = iota((BLOCK, LANES), 1) - STRIP
        spot = (at == r) | (at == r + row_blocks) | (at == r + 2 * row_blocks)
        old = lhs[r, :, LANES:].astype(F32)
        lhs[r, :, LANES:] = jnp.where(spot, rowtile[...], old).astype(BF16)
        left = lhs[r]
        for k in range(slot_count):
            z = dot(left, rhs[slot_block(r, k)])
            highest = jnp.max(z, axis=0, keepdims=True)
            e = jnp.exp2(z - highest)
            plan[r * slot_count + k] = e
            total = jnp.sum(e, axis=0, keepdims=True)
            peaks[r, k : k + 1, :] = highest
            slots[r, k : k + 1, :] = highest + jnp.log2(total)
        return carry

    for part in range(row_parts):
        rows = slice(part * part_rows, (part + 1) * part_rows)
        others(n_tgt, me_t, lambda p: first_copy(part, p, p).wait_recv())
        row_lse = first_in[part]
        top = jnp.max(row_lse, axis=0)
        total = jnp.sum(jnp.exp2(row_lse - top[None]), axis=0)
        for i in range(part_rows):
            r = part * part_rows + i
            u_ref[r : r + 1, :] = (
                jnp.log2(smass_ref[:, r * BLOCK : (r + 1) * BLOCK])
                - top[i : i + 1, :]
                - jnp.log2(total[i : i + 1, :])
            )
        strips = jnp.concatenate(
            [
                jnp.zeros((STRIP, BLOCK), F32),
                *split3(u_ref[...]),
                jnp.zeros((LANES - STRIP - 3 * row_blocks, BLOCK), F32),
            ],
            axis=0,
        )
        rowtile[...] = strips.T
        lax.fori_loop(part * part_rows, (part + 1) * part_rows, first_columns, 0)

    def slot_parts():
        lines = slots[...].reshape(all_slots, BLOCK)
        parts = [*split3(lines)]
        if 3 * all_slots < DEPTH:
            parts.append(jnp.zeros((DEPTH - 3 * all_slots, BLOCK), F32))
        return jnp.concatenate(parts, axis=0).astype(BF16)

    def send_columns(phase, lines):
        for s in range(owners):
            cols_out[phase, s] = lines[s * own_blocks : (s + 1) * own_blocks, :]
        others(n_src, me_s, lambda p: col_copy(phase, p, me_s).start())
        cols_in[phase, me_s] = cols_out[phase, owner]

    def wait_columns(phase):
        others(n_src, me_s, lambda p: col_copy(phase, p, p).wait_recv())
        return cols_in[phase]

    def send_back(phase, lines):
        back[phase, owner] = lines
        others(owners, owner, lambda p: back_copy(phase, p, owner).start())

    def wait_back(phase):
        others(owners, owner, lambda p: back_copy(phase, p, p).wait_recv())

    present = dot(hot[...], jnp.where(iota((DEPTH, BLOCK), 0) < all_slots, 1.0, 0.0).astype(BF16))
    by_row = jnp.where(present > 0.5, dot(hot[...], slot_parts()), ABSENT)
    by_row = by_row.reshape(row_blocks, col_blocks, BLOCK)
    top = jnp.max(by_row, axis=0)
    send_columns(0, top + jnp.log2(jnp.sum(jnp.exp2(by_row - top[None]), axis=0)))

    own_width = own_blocks * BLOCK
    tmass = tmass_ref[:, pl.ds(pl.multiple_of(owner * own_width, own_width), own_width)]
    tmass = jnp.concatenate(
        [tmass[:, j * BLOCK : (j + 1) * BLOCK] for j in range(own_blocks)], axis=0
    )
    tmass_log = jnp.log2(tmass)
    loads[4].wait()

    def feature_side(b, carry):
        feats[b, :feat, :] = feat_ref[:, pl.ds(pl.multiple_of(b * BLOCK, BLOCK), BLOCK)]
        feats[b, feat:, :] = jnp.ones((feats.shape[1] - feat, BLOCK), BF16)
        return carry

    lax.fori_loop(0, col_blocks, feature_side, 0)

    col_lse = wait_columns(0)
    top = jnp.max(col_lse, axis=0)
    total = jnp.sum(jnp.exp2(col_lse - top[None]), axis=0)
    send_back(0, tmass_log - top - jnp.log2(total))
    snorm = []
    for r in range(row_blocks):
        x = src_ref[:, r * BLOCK : (r + 1) * BLOCK].astype(F32)
        snorm.append(jnp.sum(x * x, axis=0, keepdims=True))
    wait_back(0)

    def back_line(phase, b):
        return back[phase, b // own_blocks, pl.ds(b % own_blocks, 1), :]

    def second_rows(r, carry):
        total = None
        for k in range(slot_count):
            factor = jnp.exp2(peaks[r, k : k + 1, :] + back_line(0, kb_ref[r, k]))
            factors[r, k : k + 1, :] = factor
            e = plan[r * slot_count + k] * factor
            e = e[:, :LANES] + e[:, LANES:]
            total = e if total is None else total + e
        second_out[pl.ds(r, 1), :] = jnp.sum(total.T, axis=0, keepdims=True)
        return carry

    lax.fori_loop(0, row_blocks, second_rows, 0)
    others(n_tgt, me_t, lambda p: second_copy(p, me_t).start())
    second_in[me_t] = second_out[...]
    snorm = jnp.concatenate(snorm, axis=0)
    smass = jnp.concatenate(
        [smass_ref[:, r * BLOCK : (r + 1) * BLOCK] for r in range(row_blocks)], axis=0
    )
    others(n_tgt, me_t, lambda p: second_copy(p, p).wait_recv())
    row_factor = smass / jnp.sum(second_in[...], axis=0)
    rowtile[...] = jnp.concatenate(
        [row_factor, jnp.zeros((LANES - row_blocks, BLOCK), F32)], axis=0
    ).T

    def second_columns(r, carry):
        at = iota((BLOCK, LANES), 1)
        factor = jnp.sum(jnp.where(at == r, rowtile[...], 0.0), axis=1, keepdims=True)
        for k in range(slot_count):
            e = plan[r * slot_count + k]
            slots[r, k : k + 1, :] = factors[r, k : k + 1, :] * jnp.sum(
                e * factor, axis=0, keepdims=True
            )
        return carry

    lax.fori_loop(0, row_blocks, second_columns, 0)
    send_columns(1, dot(member[...], slot_parts()))
    source_potential = (EPSILON * LN2) * (u_ref[...] + jnp.log2(row_factor)) + snorm
    for r in range(row_blocks):
        spot_ref[:, r * BLOCK : (r + 1) * BLOCK] = source_potential[r : r + 1, :]
    send_back(1, tmass / jnp.sum(wait_columns(1), axis=0))
    wait_back(1)

    def pair_copy(step):
        return pltpu.make_async_remote_copy(
            src_ref=pair_out.at[step],
            dst_ref=pair_in.at[step],
            send_sem=pair_send.at[step],
            recv_sem=pair_recv.at[step],
            device_id={"tgt": chip * 2 + 1 - core},
            device_id_type=MESH,
        )

    def final_copy(step, r, origin):
        return pltpu.make_async_remote_copy(
            src_ref=pair_own.at[step],
            dst_ref=final_in.at[origin],
            send_sem=final_send.at[step],
            recv_sem=final_recv.at[origin],
            device_id={"tgt": r * 2 + core},
            device_id_type=MESH,
        )

    diagonal = iota((half, LANES), 0) == iota((half, LANES), 1)

    def weigh(step, r):
        highest = None
        scales = []
        for k in range(slot_count):
            scales.append(factors[r, k : k + 1, :] * back_line(1, kb_ref[r, k]))
            w = plan[r * slot_count + k] * scales[k]
            peak = jnp.maximum(w[:, :LANES], w[:, LANES:])
            highest = peak if highest is None else jnp.maximum(highest, peak)
        top = jnp.maximum(jnp.max(highest, axis=1, keepdims=True), TINY)
        scale = 1.0 / top
        total = None
        for k in range(slot_count):
            w = (plan[r * slot_count + k] * scales[k] * scale).astype(BF16)
            part = dot_nt(w, feats[kb_ref[r, k]])
            total = part if total is None else total + part
        total = total * top
        for h in range(2):
            sums = total[h * half : (h + 1) * half]
            den = jnp.sum(jnp.where(diagonal, sums[:, LANES:], 0.0), axis=0, keepdims=True)
            rowtile[h * half : (h + 1) * half, :] = sums[:, :LANES]
            dens[h] = jnp.broadcast_to(den, (8, LANES))

        own = pl.ds(pl.multiple_of(core * half, half), half)
        other = pl.ds(pl.multiple_of((1 - core) * half, half), half)
        pair_out[step, :half, :] = rowtile[other, :]
        pair_out[step, half:, :] = dens[1 - core]
        pair_copy(step).start()
        pair_own[step, :half, :] = rowtile[own, :]
        pair_own[step, half:, :] = dens[core]

    def share(step):
        return (chip + 1 + step) % row_blocks

    def forward(step):
        pair_copy(step).wait_recv()
        pair_own[step] = pair_own[step] + pair_in[step]
        final_copy(step, share(step), chip).start()

    last = row_blocks - 1
    for step in range(LAG):
        weigh(step, share(step))

    def project(step, carry):
        weigh(step, share(step))
        forward(step - LAG)
        return carry

    lax.fori_loop(LAG, row_blocks, project, 0)
    for step in range(row_blocks - LAG, last):
        forward(step)
    pair_copy(last).wait_recv()
    total = pair_own[last] + pair_in[last]

    def target_out(s, carry):
        for j in range(own_blocks):
            v = back[0, s, j : j + 1, :] + jnp.log2(back[1, s, j : j + 1, :])
            norm = norms[s, j : j + 1, :]
            at = pl.ds(pl.multiple_of((s * own_blocks + j) * BLOCK, BLOCK), BLOCK)
            tpot_ref[:, at] = (EPSILON * LN2) * (v - SCALE * norm) + norm
        return carry

    lax.fori_loop(0, owners, target_out, 0)

    for phase in range(2):
        others(n_src, me_s, lambda p: col_copy(phase, p, me_s).wait_send())
        others(owners, owner, lambda p: back_copy(phase, p, owner).wait_send())
    for part in range(row_parts):
        others(n_tgt, me_t, lambda p: first_copy(part, p, me_t).wait_send())
    others(n_tgt, me_t, lambda p: second_copy(p, me_t).wait_send())

    def collect(step, total):
        origin = share(step)
        final_copy(step, origin, origin).wait_recv()
        return total + final_in[origin]

    sums_ref[...] = lax.fori_loop(0, last, collect, total)

    def drain(step, carry):
        pair_copy(step).wait_send()
        final_copy(step, share(step), chip).wait_send()
        return carry

    lax.fori_loop(0, last, drain, 0)
    pair_copy(last).wait_send()


def finish(sums_ref, spot_in, tpot_in, proj_ref, spot_ref, tpot_ref):
    rows, lanes = proj_ref.shape
    diagonal = iota((rows, lanes), 0) == iota((rows, lanes), 1)
    den = jnp.sum(jnp.where(diagonal, sums_ref[rows : rows + 1, :], 0.0), axis=1, keepdims=True)
    proj_ref[...] = sums_ref[:rows, :] / den
    spot_ref[...] = spot_in[...]
    tpot_ref[...] = tpot_in[...]


def shards(n_src, n_tgt, src_emb, tgt_emb, features, src_mass, tgt_mass, kept_blocks, kept_count):
    src_rows, tgt_rows = src_emb.shape[1], tgt_emb.shape[1]
    row_blocks, col_blocks = src_rows // BLOCK, tgt_rows // BLOCK
    slot_count = kept_blocks.shape[1]
    owners = n_src // PLANES
    own_blocks = col_blocks // owners
    share_rows = src_rows // n_tgt
    feat = features.shape[0]
    part_rows = row_blocks // ROW_PARTS
    vmem = pl.BlockSpec(memory_space=pltpu.VMEM)
    anywhere = pl.BlockSpec(memory_space=pl.ANY)
    message = (row_blocks, share_rows + 8, LANES)
    dma = pltpu.SemaphoreType.DMA
    operands = (
        kept_blocks,
        kept_count.reshape(1, row_blocks),
        src_emb,
        tgt_emb,
        features,
        src_mass.reshape(1, src_rows),
        tgt_mass.reshape(1, tgt_rows),
    )
    landing = [
        (pltpu.SMEM if x.dtype == jnp.int32 else pltpu.VMEM)(x.shape, x.dtype) for x in operands
    ]
    out_lines = (
        jax.ShapeDtypeStruct((1, src_rows), F32),
        jax.ShapeDtypeStruct((1, tgt_rows), F32),
    )
    results = pl.pallas_call(
        functools.partial(kernel, n_src, n_tgt),
        out_shape=(jax.ShapeDtypeStruct((share_rows + 8, feat), F32), *out_lines),
        in_specs=[anywhere] * 7,
        out_specs=(vmem, vmem, vmem),
        scratch_shapes=[
            *landing,
            pltpu.VMEM((row_blocks, BLOCK, DEPTH), BF16),
            pltpu.VMEM((col_blocks + 1, DEPTH, BLOCK), BF16),
            pltpu.VMEM((col_blocks, 2 * LANES, BLOCK), BF16),
            pltpu.VMEM((slot_count, BLOCK, BLOCK), F32),
            pltpu.VMEM((row_blocks * slot_count, BLOCK, BLOCK), F32),
            pltpu.VMEM((row_blocks * col_blocks, DEPTH), BF16),
            pltpu.VMEM((col_blocks, DEPTH), BF16),
            pltpu.VMEM((row_blocks, slot_count, BLOCK), F32),
            pltpu.VMEM((row_blocks, slot_count, BLOCK), F32),
            pltpu.VMEM((row_blocks, slot_count, BLOCK), F32),
            pltpu.VMEM((owners, own_blocks, BLOCK), F32),
            pltpu.VMEM((row_blocks, BLOCK), F32),
            pltpu.VMEM((ROW_PARTS, part_rows, BLOCK), F32),
            pltpu.VMEM((ROW_PARTS, n_tgt, part_rows, BLOCK), F32),
            pltpu.VMEM((row_blocks, BLOCK), F32),
            pltpu.VMEM((n_tgt, row_blocks, BLOCK), F32),
            pltpu.VMEM((2, owners, own_blocks, BLOCK), F32),
            pltpu.VMEM((2, n_src, own_blocks, BLOCK), F32),
            pltpu.VMEM((2, owners, own_blocks, BLOCK), F32),
            pltpu.VMEM((BLOCK, LANES), F32),
            pltpu.VMEM((2, 8, LANES), F32),
            pltpu.VMEM(message, F32),
            pltpu.VMEM(message, F32),
            pltpu.VMEM(message, F32),
            pltpu.VMEM(message, F32),
            dma((7,)),
            dma((ROW_PARTS, n_tgt)),
            dma((ROW_PARTS, n_tgt)),
            dma((n_tgt,)),
            dma((n_tgt,)),
            dma((2, n_src)),
            dma((2, n_src)),
            dma((2, owners)),
            dma((2, owners)),
            dma((row_blocks,)),
            dma((row_blocks,)),
            dma((row_blocks,)),
            dma((row_blocks,)),
        ],
        compiler_params=pltpu.CompilerParams(
            collective_id=0, has_side_effects=True, vmem_limit_bytes=56 * 1024 * 1024
        ),
        name="transport",
    )(*operands)
    projected, src_potential, tgt_potential = pl.pallas_call(
        finish,
        out_shape=(jax.ShapeDtypeStruct((share_rows, feat), F32), *out_lines),
        in_specs=[vmem] * 3,
        out_specs=(vmem,) * 3,
        name="finish",
    )(*results)
    return projected, src_potential.reshape(src_rows), tgt_potential.reshape(tgt_rows)


def solution(mesh):
    return jax.shard_map(
        functools.partial(shards, mesh.shape["src"], mesh.shape["tgt"]),
        mesh=mesh,
        in_specs=(
            P(None, "src"),
            P(None, "tgt"),
            P(None, "tgt"),
            P("src"),
            P("tgt"),
            P("src", "tgt"),
            P("src", "tgt"),
        ),
        out_specs=(P(("src", "tgt"), None), P("src"), P("tgt")),
        check_vma=False,
    )
```
